256 devices in a mesh: replica: 64 (over x, z_lo, y), fsdp: 4 (over z_hi, core).
Axes of the slice: x: 4, y: 4, z: 8 (z_hi: 2, z_lo: 4; z = z_hi * 4 + z_lo), core: 2. Of those that a mesh axis runs over, the one named last changes fastest.
Arguments:
- activations: bfloat16 [65536, 8192], P(('replica', 'fsdp')), may hold values from -6 to 6
- key_weight: bfloat16 [64, 8192, 512], P('replica', 'fsdp'), may hold values from -0.0625 to 0.0625
- key_cotangent: bfloat16 [65536, 512], P(('replica', 'fsdp')), may hold values from -0.5 to 0.5
- grad_codes: bfloat16 [64, 28672, 128], P('replica', 'fsdp'), may hold values from -1 to 1
- grad_scales: bfloat16 [64, 28672], P('replica', 'fsdp'), may hold values from 0.099609375 to 1
- master: float32 [28672, 128], P(('fsdp', 'replica')), may hold values from -5 to 5
- momentum: float32 [28672, 128], P(('fsdp', 'replica')), may hold values from -0.75 to 0.75
Outputs:
- key_rows: bfloat16 [65536, 512], P(('replica', 'fsdp'))
- weight_grad: bfloat16 [64, 8192, 512], P('replica', 'fsdp')
- new_master: float32 [28672, 128], P(('fsdp', 'replica'))
- new_momentum: float32 [28672, 128], P(('fsdp', 'replica'))
- new_codes: bfloat16 [28672, 128], P('fsdp')
- new_scales: bfloat16 [28672], P('fsdp')
The draws below stay inside these ranges and needn't reach their ends.
All inputs are finite; a program needn't handle non-finite values. Where the reference program divides by a largest or mean magnitude, that divisor is 1e-20 or more.
Results may differ from the reference program's by a relative error of at most 0.013.
Values may be sent and summed in bfloat16 or wider, within the bound.
A program may use at most 128 MiB of HBM per device.

```python
import math
import jax
import jax.numpy as jnp
from jax import lax

D = 8192
KV_HEADS = 4
HEAD = 128
GROUP = 128
TOK_DEV = 256
KW = 512
TOKENS = 65536
GROUPS = 28672
N_REPLICA = 64
N_FSDP = 4


def draw_master(key, part):
    key = jax.random.fold_in(key, 11)
    first, second, third = jax.random.split(key, 3)
    base = jnp.clip(jax.random.normal(first, (GROUPS, GROUP), jnp.float32), -5.0, 5.0)
    row_scale = jnp.exp(jax.random.uniform(second, (GROUPS, 1), jnp.float32, math.log(0.01), math.log(0.1)))
    column_scale = jnp.exp(jax.random.uniform(third, (1, GROUP), jnp.float32, 0.0, math.log(10.0)))
    return base * row_scale * column_scale


def block_scale(own_key, extent, shards, smallest, largest):
    def one(dim, parts):
        heights = jax.random.uniform(jax.random.fold_in(jax.random.fold_in(own_key, 6), dim), (parts,), jnp.float32, smallest / len(shards), largest / len(shards))
        return jnp.repeat(jnp.exp(heights), extent[dim] // parts).reshape((-1,) + (1,) * (len(extent) - dim - 1))

    loudness = one(*shards[0])
    for cut in shards[1:]:
        loudness = loudness * one(*cut)
    return loudness


def centred(rng, extent, spread, reach, cuts=(), kind=jnp.bfloat16):
    factor_of = block_scale(rng, extent, cuts, -0.22, 0.18) if cuts else 1.0
    array = jax.random.normal(rng, extent, jnp.float32) * spread * factor_of
    return jnp.minimum(jnp.maximum(array, -reach), reach).astype(kind)


def setup_inputs(seed: int = 0) -> dict:
    streams_of = jax.random.split(jax.random.key(seed), 8)
    return {
        "activations": centred(streams_of[0], (TOKENS, D), 1.0, 6.0, ((0, 256),)),
        "key_weight": centred(streams_of[1], (N_REPLICA, D, KW), D ** -0.5, 0.0625, ((0, 64), (1, 4))),
        "key_cotangent": centred(streams_of[2], (TOKENS, KW), (1.0 / (N_FSDP * TOK_DEV) ** 0.5), 0.5, ((0, 256),)),
        "grad_codes": jnp.clip(jax.random.uniform(streams_of[3], (N_REPLICA, GROUPS, GROUP), jnp.float32, -1.0, 1.0) * block_scale(streams_of[3], (N_REPLICA, GROUPS, GROUP), ((0, 64), (1, 4)), -0.4, 0.0), -1.0, 1.0).astype(jnp.bfloat16),
        "grad_scales": jnp.clip(jnp.exp(math.log(1.0) - 2.306499 * jax.random.uniform(streams_of[4], (N_REPLICA, GROUPS), jnp.float32) ** block_scale(streams_of[4], (N_REPLICA, GROUPS), ((0, 64), (1, 4)), -0.2, 0.2)), 0.099609375, 1.0).astype(jnp.bfloat16),
        "master": draw_master(jax.random.fold_in(streams_of[7], 71), 0),
        "momentum": centred(streams_of[6], (GROUPS, GROUP), 0.05, 0.75, ((0, 256),), jnp.float32),
    }


def reference(activations, key_weight, key_cotangent, grad_codes, grad_scales, master, momentum):
    key_width = KV_HEADS * HEAD
    inputs_all = activations.reshape(N_REPLICA, N_FSDP, TOK_DEV, D)
    cotangents = key_cotangent.reshape(N_REPLICA, N_FSDP, TOK_DEV, key_width)

    def one_replica(replica_inputs):
        inputs_r, cotangents_r, weight_r = replica_inputs
        keys_r = jnp.dot(inputs_r.reshape(N_FSDP * TOK_DEV, D), weight_r, preferred_element_type=jnp.float32).astype(jnp.bfloat16)
        summed = jnp.zeros((D, key_width), jnp.float32)
        for block_index in range(N_FSDP):
            product = jnp.dot(inputs_r[block_index].T, cotangents_r[block_index], preferred_element_type=jnp.float32)
            product = lax.optimization_barrier(product.astype(jnp.bfloat16))
            summed = summed + product.astype(jnp.float32)
        return keys_r, summed.astype(jnp.bfloat16)

    key_rows, weight_grad = lax.map(one_replica, (inputs_all, cotangents, key_weight))
    key_rows = key_rows.reshape(TOKENS, key_width)

    def add_replica(replica_index, summed):
        codes_r = grad_codes[replica_index].astype(jnp.float32)
        scales_r = grad_scales[replica_index].astype(jnp.float32)
        return summed + codes_r * scales_r[:, None]

    summed = lax.fori_loop(0, N_REPLICA, add_replica, jnp.zeros((GROUPS, GROUP), jnp.float32))
    outer_grad = summed / N_REPLICA
    new_momentum = 0.9 * momentum + outer_grad
    new_master = master - 0.7 * (outer_grad + 0.9 * new_momentum)
    new_scales = (jnp.max(jnp.abs(new_master), axis=1) + 1e-6).astype(jnp.bfloat16)
    new_codes = (new_master / new_scales.astype(jnp.float32)[:, None]).astype(jnp.bfloat16)
    return (key_rows, weight_grad, new_master, new_momentum, new_codes, new_scales)
```

```python
import jax
import jax.numpy as jnp
from jax import lax
from jax.experimental import pallas as pl
from jax.experimental.pallas import tpu as pltpu
from jax.sharding import PartitionSpec as P

MESH = pl.DeviceIdType.MESH
F32, BF16 = jnp.float32, jnp.bfloat16

TOK, DEPTH, KW = 256, 2048, 512
CODE_ROWS, OWN = 7168, 112
QUARTER = CODE_ROWS // 4
CHUNKS = ((0, 64), (64, 64), (128, 64), (192, 64))
NQ = len(CHUNKS)


def kernel(
    act, weight, cot, codes, scales, master, momentum,
    key_out, grad_out, master_out, momentum_out, codes_out, scales_out,
    x_loc, x_rem, c_loc, c_rem, w_v, codes_v, scales_v, master_v, momentum_v,
    p_loc, p_sib, p_rem, p_ex, ret_s, ret_r, grad_f, grad_b, key_b,
    prod, recv_x, s_y, recv_y, s_z, recv_z, gath, nm_v, nmom_v,
    sem_in, sem_xs, sem_xr, sem_sib_s, sem_sib_r, sem_ex_s, sem_ex_r, sem_ret_s, sem_ret_r,
    sem_rs_s, sem_rs_r, sem_ag_s, sem_ag_r, sem_out,
):
    r = lax.axis_index("replica")
    f = lax.axis_index("fsdp")
    x, zl, y = r // 16, (r // 4) % 4, r % 4
    zh, c = f // 2, f % 2
    sib = (r, zh * 2 + (1 - c))
    far = [(r, (1 - zh) * 2 + k) for k in range(2)]
    far_same = (r, (1 - zh) * 2 + c)
    px = [(((x + k) % 4) * 16 + zl * 4 + y, f) for k in range(1, 4)]
    pz = [(x * 16 + ((zl + k) % 4) * 4 + y, f) for k in range(1, 4)]
    py = [(x * 16 + zl * 4 + (y + k) % 4, f) for k in range(1, 4)]

    def columns(owner):
        return pl.ds(pl.multiple_of(owner * DEPTH, DEPTH), DEPTH)

    def remote(src, dst, ssem, rsem, to):
        copy = pltpu.make_async_remote_copy(src, dst, ssem, rsem, device_id=to, device_id_type=MESH)
        copy.start()
        return copy

    def local_copy(src, dst, sem):
        copy = pltpu.make_async_copy(src, dst, sem)
        copy.start()
        return copy

    in_codes = local_copy(codes, codes_v, sem_in.at[0])
    in_scales = local_copy(scales, scales_v, sem_in.at[1])
    in_x = local_copy(act.at[:, columns(f)], x_loc.at[pl.ds(0, TOK)], sem_in.at[2])
    in_w = local_copy(weight, w_v, sem_in.at[3])
    in_c = local_copy(cot, c_loc.at[pl.ds(0, TOK)], sem_in.at[4])
    in_master = local_copy(master, master_v, sem_in.at[5])
    in_momentum = local_copy(momentum, momentum_v, sem_in.at[6])

    peers = [sib] + far + px + py + pz
    barrier = pltpu.get_barrier_semaphore()
    for peer in peers:
        pl.semaphore_signal(barrier, inc=1, device_id=peer, device_id_type=MESH)
    pl.semaphore_wait(barrier, len(peers))

    far_x = []
    for q, (start, rows) in enumerate(CHUNKS):
        for k in range(2):
            far_x.append(remote(
                act.at[pl.ds(start, rows), columns((1 - zh) * 2 + k)],
                x_rem.at[pl.ds(2 * start + c * rows, rows)],
                sem_xs.at[2 * q + k], sem_xr.at[2 * q + c], far[k],
            ))
    far_c = remote(cot, c_rem.at[pl.ds(c * TOK, TOK)], sem_sib_s.at[2], sem_sib_r.at[2], far_same)
    sib_x = remote(act.at[:, columns(zh * 2 + (1 - c))], x_loc.at[pl.ds(TOK, TOK)], sem_sib_s.at[0], sem_sib_r.at[0], sib)
    sib_c = remote(cot, c_loc.at[pl.ds(TOK, TOK)], sem_sib_s.at[1], sem_sib_r.at[1], sib)

    in_codes.wait()
    in_scales.wait()
    eye = lax.broadcasted_iota(jnp.int32, (128, 128), 0) == lax.broadcasted_iota(jnp.int32, (128, 128), 1)
    rs_x = []
    for k in (1, 3, 2, 0):
        base = ((x + k) % 4) * QUARTER

        def term(b, carry, k=k, base=base):
            at = pl.multiple_of(base + b * 128, 128)
            row = scales_v[:, pl.ds(at, 128)].astype(F32)
            diagonal = jnp.where(eye, jnp.broadcast_to(row, (128, 128)), 0.0).astype(BF16)
            block = jnp.dot(diagonal, codes_v[pl.ds(at, 128), :], preferred_element_type=F32)
            prod[k, pl.ds(pl.multiple_of(b * 128, 128), 128), :] = block.astype(BF16)
            return carry

        lax.fori_loop(0, QUARTER // 128, term, 0)
        if k:
            rs_x.append(remote(prod.at[k], recv_x.at[k - 1], sem_rs_s.at[k - 1], sem_rs_r.at[k - 1], px[k - 1]))

    in_x.wait()
    in_w.wait()
    in_c.wait()
    sib_x.wait()
    sib_c.wait()

    def keys_local(b, carry):
        at = pl.ds(pl.multiple_of(b * 128, 128), 128)
        p_loc[at, :] = jnp.dot(x_loc[at, :], w_v[...], preferred_element_type=F32)
        return carry

    lax.fori_loop(0, 2 * TOK // 128, keys_local, 0)
    sib_p = remote(p_loc.at[pl.ds(TOK, TOK)], p_sib, sem_sib_s.at[3], sem_sib_r.at[3], sib)

    def transposed_dot(lhs, rhs):
        return lax.dot_general(lhs, rhs, (((0,), (0,)), ((), ())), preferred_element_type=F32)

    def grad_local(b, carry):
        at = pl.ds(pl.multiple_of(b * 256, 256), 256)
        grad_f[at, :] = transposed_dot(x_loc[:, at], c_loc[...])
        return carry

    lax.fori_loop(0, DEPTH // 256, grad_local, 0)

    for copy in rs_x:
        copy.wait()

    def sum_x(b, carry):
        at = pl.ds(pl.multiple_of(b * OWN, 16), OWN)
        total = prod[0, at, :].astype(F32)
        for k in range(3):
            total += recv_x[k, at, :].astype(F32)
        s_y[b // 4, b % 4] = total.astype(BF16)
        return carry

    lax.fori_loop(0, 16, sum_x, 0)
    rs_y = [
        remote(s_y.at[:, (y + k) % 4], recv_y.at[k - 1], sem_rs_s.at[2 + k], sem_rs_r.at[2 + k], py[k - 1])
        for k in range(1, 4)
    ]
    for copy in rs_y:
        copy.wait()

    def sum_y(b, carry):
        total = s_y[b, y].astype(F32)
        for k in range(3):
            total += recv_y[k, b].astype(F32)
        s_z[b] = total.astype(BF16)
        return carry

    lax.fori_loop(0, 4, sum_y, 0)
    rs_z = [
        remote(s_z.at[(zl + k) % 4], recv_z.at[k - 1], sem_rs_s.at[5 + k], sem_rs_r.at[5 + k], pz[k - 1])
        for k in range(1, 4)
    ]
    in_master.wait()
    in_momentum.wait()
    for copy in rs_z:
        copy.wait()

    total = s_z[zl].astype(F32)
    for k in range(3):
        total += recv_z[k].astype(F32)
    outer = total / 64
    new_momentum = 0.9 * momentum_v[...] + outer
    new_master = master_v[...] - 0.7 * (outer + 0.9 * new_momentum)
    nmom_v[...] = new_momentum
    nm_v[...] = new_master
    largest = jnp.max(jnp.abs(new_master), axis=1, keepdims=True)
    scale = (largest + 1e-06).astype(BF16).astype(F32)
    gath[x, zl, y, 0:OWN, :] = (new_master / scale).astype(BF16)
    corner = lax.broadcasted_iota(jnp.int32, (OWN, 128), 0) == lax.broadcasted_iota(jnp.int32, (OWN, 128), 1)
    row = jnp.sum(jnp.where(corner, jnp.broadcast_to(scale, (OWN, 128)), 0.0), axis=0, keepdims=True)
    gath[x, zl, y, OWN:128, :] = jnp.broadcast_to(row, (128 - OWN, 128)).astype(BF16)
    out_master = local_copy(nm_v, master_out, sem_out.at[0])
    out_momentum = local_copy(nmom_v, momentum_out, sem_out.at[1])

    ag_z = [
        remote(gath.at[x, zl, y], gath.at[x, zl, y], sem_ag_s.at[k - 1], sem_ag_r.at[k - 1], pz[k - 1])
        for k in range(1, 4)
    ]
    for copy in ag_z:
        copy.wait()
    ag_y = [
        remote(gath.at[x, :, y], gath.at[x, :, y], sem_ag_s.at[2 + k], sem_ag_r.at[2 + k], py[k - 1])
        for k in range(1, 4)
    ]
    for copy in ag_y:
        copy.wait()
    ag_x = [
        remote(gath.at[x], gath.at[x], sem_ag_s.at[5 + k], sem_ag_r.at[5 + k], px[k - 1])
        for k in range(1, 4)
    ]

    def keys_far(q):
        start, rows = CHUNKS[q]
        for k in range(2):
            far_x[2 * q + k].wait_send()
        for k in range(2):
            pltpu.make_async_copy(
                x_rem.at[pl.ds(2 * start + k * rows, rows)], x_rem.at[pl.ds(2 * start + k * rows, rows)],
                sem_xr.at[2 * q + k],
            ).wait()
        both = pl.ds(2 * start, 2 * rows)
        p_rem[both, :] = jnp.dot(x_rem[both, :], w_v[...], preferred_element_type=F32)
        return remote(
            p_rem.at[pl.ds(2 * start + (1 - c) * rows, rows)], p_ex.at[pl.ds(start, rows)],
            sem_ex_s.at[q], sem_ex_r.at[q], sib,
        )

    def keys_back(q, exchange):
        start, rows = CHUNKS[q]
        exchange.wait()
        at = pl.ds(start, rows)
        mine = p_rem[pl.ds(pl.multiple_of(2 * start + c * rows, rows), rows), :]
        ret_s[at, :] = (mine + p_ex[at, :]).astype(BF16)
        return remote(ret_s.at[at], ret_r.at[at], sem_ret_s.at[q], sem_ret_r.at[q], far_same)

    returned = []
    for q in range(NQ - 1):
        exchange = keys_far(q)
        returned.append(keys_back(q, exchange))

    for copy in ag_x:
        copy.wait()
    out_codes = local_copy(gath.at[:, :, :, pl.ds(0, OWN)], codes_out, sem_out.at[2])
    out_scales = local_copy(gath.at[:, :, :, pl.ds(OWN, 16)], scales_out, sem_out.at[3])

    exchange = keys_far(NQ - 1)
    far_c.wait()
    share_c = remote(
        c_rem.at[pl.ds(c * TOK, TOK)], c_rem.at[pl.ds(c * TOK, TOK)], sem_sib_s.at[4], sem_sib_r.at[4], sib
    )
    returned.append(keys_back(NQ - 1, exchange))
    sib_p.wait()
    share_c.wait()

    def grad_far(b, carry):
        at = pl.ds(pl.multiple_of(b * 256, 256), 256)
        total = grad_f[at, :]
        for q, (start, rows) in enumerate(CHUNKS):
            for k in range(2):
                total += transposed_dot(x_rem[pl.ds(2 * start + k * rows, rows), at], c_rem[pl.ds(k * TOK + start, rows), :])
        grad_b[at, :] = total.astype(BF16)
        return carry

    lax.fori_loop(0, DEPTH // 256, grad_far, 0)
    out_grad = local_copy(grad_b, grad_out, sem_out.at[4])

    for q, (start, rows) in enumerate(CHUNKS):
        returned[q].wait()
        at = pl.ds(start, rows)
        key_b[at, :] = (p_loc[at, :] + p_sib[at, :] + ret_r[at, :].astype(F32)).astype(BF16)
    out_key = local_copy(key_b, key_out, sem_out.at[5])
    for copy in (out_master, out_momentum, out_codes, out_scales, out_grad, out_key):
        copy.wait()


def local(activations, key_weight, key_cotangent, grad_codes, grad_scales, master, momentum):
    anywhere = pl.BlockSpec(memory_space=pl.ANY)
    dma = pltpu.SemaphoreType.DMA
    key_rows, weight_grad, new_master, new_momentum, codes, scales = pl.pallas_call(
        kernel,
        out_shape=(
            jax.ShapeDtypeStruct((TOK, KW), BF16),
            jax.ShapeDtypeStruct((DEPTH, KW), BF16),
            jax.ShapeDtypeStruct((OWN, 128), F32),
            jax.ShapeDtypeStruct((OWN, 128), F32),
            jax.ShapeDtypeStruct((4, 4, 4, OWN, 128), BF16),
            jax.ShapeDtypeStruct((4, 4, 4, 16, 128), BF16),
        ),
        in_specs=[anywhere] * 7,
        out_specs=(anywhere,) * 6,
        scratch_shapes=[
            pltpu.VMEM((2 * TOK, DEPTH), BF16),
            pltpu.VMEM((2 * TOK, DEPTH), BF16),
            pltpu.VMEM((2 * TOK, KW), BF16),
            pltpu.VMEM((2 * TOK, KW), BF16),
            pltpu.VMEM((DEPTH, KW), BF16),
            pltpu.VMEM((CODE_ROWS, 128), BF16),
            pltpu.VMEM((1, CODE_ROWS), BF16),
            pltpu.VMEM((OWN, 128), F32),
            pltpu.VMEM((OWN, 128), F32),
            pltpu.VMEM((2 * TOK, KW), F32),
            pltpu.VMEM((TOK, KW), F32),
            pltpu.VMEM((2 * TOK, KW), F32),
            pltpu.VMEM((TOK, KW), F32),
            pltpu.VMEM((TOK, KW), BF16),
            pltpu.VMEM((TOK, KW), BF16),
            pltpu.VMEM((DEPTH, KW), F32),
            pltpu.VMEM((DEPTH, KW), BF16),
            pltpu.VMEM((TOK, KW), BF16),
            pltpu.VMEM((4, QUARTER, 128), BF16),
            pltpu.VMEM((3, QUARTER, 128), BF16),
            pltpu.VMEM((4, 4, OWN, 128), BF16),
            pltpu.VMEM((3, 4, OWN, 128), BF16),
            pltpu.VMEM((4, OWN, 128), BF16),
            pltpu.VMEM((3, OWN, 128), BF16),
            pltpu.VMEM((4, 4, 4, 128, 128), BF16),
            pltpu.VMEM((OWN, 128), F32),
            pltpu.VMEM((OWN, 128), F32),
            dma((7,)),
            dma((2 * NQ,)), dma((2 * NQ,)),
            dma((5,)), dma((5,)),
            dma((NQ,)), dma((NQ,)),
            dma((NQ,)), dma((NQ,)),
            dma((9,)), dma((9,)),
            dma((9,)), dma((9,)),
            dma((6,)),
        ],
        compiler_params=pltpu.CompilerParams(
            collective_id=0, has_side_effects=True, vmem_limit_bytes=48 * 2**20
        ),
    )(activations, key_weight[0], key_cotangent, grad_codes[0], grad_scales, master, momentum)
    new_codes = codes.reshape(CODE_ROWS, 128)
    new_scales = scales[:, :, :, 0, :OWN].reshape(CODE_ROWS)
    return (key_rows, weight_grad[None], new_master, new_momentum, new_codes, new_scales)


def solution(mesh):
    return jax.shard_map(
        local,
        mesh=mesh,
        in_specs=(
            P(("replica", "fsdp"), None),
            P("replica", "fsdp", None),
            P(("replica", "fsdp"), None),
            P("replica", "fsdp", None),
            P("replica", "fsdp"),
            P(("fsdp", "replica"), None),
            P(("fsdp", "replica"), None),
        ),
        out_specs=(
            P(("replica", "fsdp"), None),
            P("replica", "fsdp", None),
            P(("fsdp", "replica"), None),
            P(("fsdp", "replica"), None),
            P("fsdp", None),
            P("fsdp"),
        ),
        check_vma=False,
    )
```

```python
import jax
import jax.numpy as jnp
from jax import lax
from jax.experimental import pallas as pl
from jax.experimental.pallas import tpu as pltpu
from jax.sharding import PartitionSpec as P

MESH = pl.DeviceIdType.MESH
F32, BF16 = jnp.float32, jnp.bfloat16

TOK, DEPTH, KW = 256, 2048, 512
CODE_ROWS, OWN = 7168, 112
QUARTER = CODE_ROWS // 4
UNIT, WINDOW = 16, 2
NU = TOK // UNIT
CHUNKS = ((0, 64), (64, 64), (128, 64), (192, 32), (224, 32))
NQ = len(CHUNKS)
ORDER = [*range(0, 4), "c", *range(4, NU)]
PUMPS = (1, 0, 1, 2, 1, 1, 1, 1, 3, 0)


def kernel(
    act, weight, cot, codes, scales, master, momentum,
    key_b, grad_b, nm_v, nmom_v, gath, scales_b,
    x_loc, x_rem, c_loc, c_rem, c_mix, w_v, codes_v, scales_v, master_v, momentum_v,
    p_loc, p_sib, p_rem, p_ex, ret_s, ret_r, grad_f,
    prod, recv_x, s_y, recv_y, s_z, recv_z,
    sem_in, sem_xs, sem_xr, sem_sib_s, sem_sib_r, sem_ex_s, sem_ex_r, sem_ret_s, sem_ret_r,
    sem_rs_s, sem_rs_r, sem_ag_s, sem_ag_r,
):
    r = lax.axis_index("replica")
    f = lax.axis_index("fsdp")
    x, zl, y = r // 16, (r // 4) % 4, r % 4
    zh, c = f // 2, f % 2
    sib = (r, zh * 2 + (1 - c))
    far = [(r, (1 - zh) * 2 + k) for k in range(2)]
    far_same = (r, (1 - zh) * 2 + c)
    px = [(((x + k) % 4) * 16 + zl * 4 + y, f) for k in range(1, 4)]
    pz = [(x * 16 + ((zl + k) % 4) * 4 + y, f) for k in range(1, 4)]
    py = [(x * 16 + zl * 4 + (y + k) % 4, f) for k in range(1, 4)]

    def columns(owner):
        return pl.ds(pl.multiple_of(owner * DEPTH, DEPTH), DEPTH)

    def remote(src, dst, ssem, rsem, to):
        copy = pltpu.make_async_remote_copy(src, dst, ssem, rsem, device_id=to, device_id_type=MESH)
        copy.start()
        return copy

    def local_copy(src, dst, sem):
        copy = pltpu.make_async_copy(src, dst, sem)
        copy.start()
        return copy

    in_codes = local_copy(codes, codes_v, sem_in.at[0])
    in_scales = local_copy(scales, scales_v, sem_in.at[1])
    in_x = local_copy(act.at[:, columns(f)], x_loc.at[pl.ds(0, TOK)], sem_in.at[2])
    in_w = local_copy(weight, w_v, sem_in.at[3])
    in_c = local_copy(cot, c_loc.at[pl.ds(0, TOK)], sem_in.at[4])
    in_master = local_copy(master, master_v, sem_in.at[5])
    in_momentum = local_copy(momentum, momentum_v, sem_in.at[6])

    peers = [sib] + far + px + py + pz
    barrier = pltpu.get_barrier_semaphore()
    for peer in peers:
        pl.semaphore_signal(barrier, inc=1, device_id=peer, device_id_type=MESH)
    pl.semaphore_wait(barrier, len(peers))

    far_x, far_c, issued = {}, [], []

    def send_far(u):
        if u == "c":
            copy = remote(cot, c_rem.at[pl.ds(c * TOK, TOK)], sem_sib_s.at[2], sem_sib_r.at[2], far_same)
            far_c.append(copy)
            return [copy]
        start, rows = next(chunk for chunk in CHUNKS if chunk[0] <= u * UNIT < sum(chunk))
        copies = []
        for k in range(2):
            copies.append(remote(
                act.at[pl.ds(u * UNIT, UNIT), columns((1 - zh) * 2 + k)],
                x_rem.at[pl.ds(start + u * UNIT + c * rows, UNIT)],
                sem_xs.at[2 * u + k], sem_xr.at[2 * u + c], far[k],
            ))
        return copies

    def pump(steps):
        for _ in range(steps):
            if len(issued) == len(ORDER):
                return
            if len(issued) >= WINDOW:
                for copy in issued[len(issued) - WINDOW]:
                    copy.wait_send()
            issued.append(send_far(ORDER[len(issued)]))

    pump(WINDOW)
    sib_x = remote(act.at[:, columns(zh * 2 + (1 - c))], x_loc.at[pl.ds(TOK, TOK)], sem_sib_s.at[0], sem_sib_r.at[0], sib)
    sib_c = remote(cot, c_loc.at[pl.ds(TOK, TOK)], sem_sib_s.at[1], sem_sib_r.at[1], sib)

    in_codes.wait()
    in_scales.wait()
    eye = lax.broadcasted_iota(jnp.int32, (128, 128), 0) == lax.broadcasted_iota(jnp.int32, (128, 128), 1)
    rs_x = []
    for k in (1, 3, 2, 0):
        base = ((x + k) % 4) * QUARTER

        def term(b, carry, k=k, base=base):
            at = pl.multiple_of(base + b * 128, 128)
            row = scales_v[:, pl.ds(at, 128)].astype(F32)
            diagonal = jnp.where(eye, jnp.broadcast_to(row, (128, 128)), 0.0).astype(BF16)
            block = jnp.dot(diagonal, codes_v[pl.ds(at, 128), :], preferred_element_type=F32)
            prod[k, pl.ds(pl.multiple_of(b * 128, 128), 128), :] = block.astype(BF16)
            return carry

        lax.fori_loop(0, QUARTER // 128, term, 0)
        if k:
            rs_x.append(remote(prod.at[k], recv_x.at[k - 1], sem_rs_s.at[k - 1], sem_rs_r.at[k - 1], px[k - 1]))
        if k in (2, 3):
            pump(PUMPS[0])

    pump(PUMPS[1])
    in_x.wait()
    in_w.wait()
    in_c.wait()
    sib_x.wait()
    sib_c.wait()

    def keys_local(b, carry):
        at = pl.ds(pl.multiple_of(b * 128, 128), 128)
        p_loc[at, :] = jnp.dot(x_loc[at, :], w_v[...], preferred_element_type=F32)
        return carry

    lax.fori_loop(0, 2 * TOK // 128, keys_local, 0)
    sib_p = remote(p_loc.at[pl.ds(TOK, TOK)], p_sib, sem_sib_s.at[3], sem_sib_r.at[3], sib)

    pump(PUMPS[2])

    def transposed_dot(lhs, rhs):
        return lax.dot_general(lhs, rhs, (((0,), (0,)), ((), ())), preferred_element_type=F32)

    def grad_local(b, carry):
        at = pl.ds(pl.multiple_of(b * 256, 256), 256)
        grad_f[at, :] = transposed_dot(x_loc[:, at], c_loc[...])
        return carry

    lax.fori_loop(0, DEPTH // 256, grad_local, 0)

    pump(PUMPS[3])
    for copy in rs_x:
        copy.wait()

    def sum_x(b, carry):
        at = pl.ds(pl.multiple_of(b * OWN, 16), OWN)
        total = prod[0, at, :].astype(F32)
        for k in range(3):
            total += recv_x[k, at, :].astype(F32)
        s_y[b // 4, b % 4] = total.astype(BF16)
        return carry

    lax.fori_loop(0, 16, sum_x, 0)
    rs_y = [
        remote(s_y.at[:, (y + k) % 4], recv_y.at[k - 1], sem_rs_s.at[2 + k], sem_rs_r.at[2 + k], py[k - 1])
        for k in range(1, 4)
    ]
    pump(PUMPS[4])
    for copy in rs_y:
        copy.wait()

    def sum_y(b, carry):
        total = s_y[b, y].astype(F32)
        for k in range(3):
            total += recv_y[k, b].astype(F32)
        s_z[b] = total.astype(BF16)
        return carry

    lax.fori_loop(0, 4, sum_y, 0)
    rs_z = [
        remote(s_z.at[(zl + k) % 4], recv_z.at[k - 1], sem_rs_s.at[5 + k], sem_rs_r.at[5 + k], pz[k - 1])
        for k in range(1, 4)
    ]
    pump(PUMPS[5])
    in_master.wait()
    in_momentum.wait()
    for copy in rs_z:
        copy.wait()

    total = s_z[zl].astype(F32)
    for k in range(3):
        total += recv_z[k].astype(F32)
    outer = total / 64
    new_momentum = 0.9 * momentum_v[...] + outer
    new_master = master_v[...] - 0.7 * (outer + 0.9 * new_momentum)
    nmom_v[...] = new_momentum
    nm_v[...] = new_master
    largest = jnp.max(jnp.abs(new_master), axis=1, keepdims=True)
    scale = (largest + 1e-06).astype(BF16).astype(F32)
    gath[x, zl, y, 0:OWN, :] = (new_master / scale).astype(BF16)
    corner = lax.broadcasted_iota(jnp.int32, (OWN, 128), 0) == lax.broadcasted_iota(jnp.int32, (OWN, 128), 1)
    row = jnp.sum(jnp.where(corner, jnp.broadcast_to(scale, (OWN, 128)), 0.0), axis=0, keepdims=True)
    gath[x, zl, y, OWN:128, :] = jnp.broadcast_to(row, (128 - OWN, 128)).astype(BF16)

    ag_z = [
        remote(gath.at[x, zl, y], gath.at[x, zl, y], sem_ag_s.at[k - 1], sem_ag_r.at[k - 1], pz[k - 1])
        for k in range(1, 4)
    ]
    pump(PUMPS[6])
    for copy in ag_z:
        copy.wait()
    ag_y = [
        remote(gath.at[x, :, y], gath.at[x, :, y], sem_ag_s.at[2 + k], sem_ag_r.at[2 + k], py[k - 1])
        for k in range(1, 4)
    ]
    pump(PUMPS[7])
    for copy in ag_y:
        copy.wait()
    ag_x = [
        remote(gath.at[x], gath.at[x], sem_ag_s.at[5 + k], sem_ag_r.at[5 + k], px[k - 1])
        for k in range(1, 4)
    ]

    pump(PUMPS[8])
    far_c[0].wait_recv()
    share_c = remote(
        c_rem.at[pl.ds(c * TOK, TOK)], c_rem.at[pl.ds(c * TOK, TOK)], sem_sib_s.at[4], sem_sib_r.at[4], sib
    )

    def pack_scales():
        lane = lax.broadcasted_iota(jnp.int32, (1, 128), 1)
        for part in range(4):
            rows = [jnp.zeros((1, 128), F32) for _ in range(QUARTER // 128)]
            for owner in range(16):
                at, shift = divmod(owner * OWN, 128)
                row = gath[part, owner // 4, owner % 4, pl.ds(OWN, 16), :][0:1].astype(F32)
                row = jnp.where(lane < OWN, row, 0.0)
                if shift:
                    row = pltpu.roll(row, shift, 1)
                rows[at] += jnp.where(lane >= shift, row, 0.0)
                if shift + OWN > 128:
                    rows[at + 1] += jnp.where(lane < shift, row, 0.0)
            for i, row in enumerate(rows):
                scales_b[pl.ds(part * (QUARTER // 128) + i, 1), :] = row

    def keys_far(q):
        start, rows = CHUNKS[q]
        for u in range(start // UNIT, (start + rows) // UNIT):
            while u not in [item for item in ORDER[:len(issued)]]:
                pump(1)
            for k in range(2):
                part = x_rem.at[pl.ds(start + u * UNIT + k * rows, UNIT)]
                pltpu.make_async_copy(part, part, sem_xr.at[2 * u + k]).wait()
        both = pl.ds(2 * start, 2 * rows)
        p_rem[both, :] = jnp.dot(x_rem[both, :], w_v[...], preferred_element_type=F32)
        return remote(
            p_rem.at[pl.ds(2 * start + (1 - c) * rows, rows)], p_ex.at[pl.ds(start, rows)],
            sem_ex_s.at[q], sem_ex_r.at[q], sib,
        )

    def keys_back(q, exchange):
        start, rows = CHUNKS[q]
        exchange.wait()
        at = pl.ds(start, rows)
        mine = p_rem[pl.ds(pl.multiple_of(2 * start + c * rows, rows), rows), :]
        ret_s[at, :] = (mine + p_ex[at, :]).astype(BF16)
        return remote(ret_s.at[at], ret_r.at[at], sem_ret_s.at[q], sem_ret_r.at[q], far_same)

    def grad_far(q):
        start, rows = CHUNKS[q]
        both = pl.ds(2 * start, 2 * rows)

        def tile(b, carry):
            at = pl.ds(pl.multiple_of(b * 256, 256), 256)
            total = grad_f[at, :] + transposed_dot(x_rem[both, at], c_mix[both, :])
            if q < NQ - 1:
                grad_f[at, :] = total
            else:
                grad_b[at, :] = total.astype(BF16)
            return carry

        lax.fori_loop(0, DEPTH // 256, tile, 0)

    exchange = keys_far(0)
    share_c.wait()
    for q, (start, rows) in enumerate(CHUNKS):
        for k in range(2):
            c_mix[pl.ds(2 * start + k * rows, rows), :] = c_rem[pl.ds(k * TOK + start, rows), :]
    returned = []
    pump(PUMPS[9])
    for q in range(NQ):
        if q == NQ - 2:
            for copy in ag_x:
                copy.wait()
            pack_scales()
        if q:
            exchange = keys_far(q)
        if q < NQ - 1:
            grad_far(q)
            pump(1)
            returned.append(keys_back(q, exchange))
            pump(1)
    returned.append(keys_back(NQ - 1, exchange))
    grad_far(NQ - 1)
    for copies in issued[-WINDOW:]:
        for copy in copies:
            copy.wait_send()
    sib_p.wait()

    for q, (start, rows) in enumerate(CHUNKS):
        returned[q].wait()
        at = pl.ds(start, rows)
        key_b[at, :] = (p_loc[at, :] + p_sib[at, :] + ret_r[at, :].astype(F32)).astype(BF16)


def write(key_v, grad_v, nm_v, nmom_v, gath, scales_v, key_out, grad_out, master_out, momentum_out, codes_out, scales_out, scales_b, sem):
    copies = [
        pltpu.make_async_copy(src, dst, sem.at[i])
        for i, (src, dst) in enumerate((
            (grad_v, grad_out),
            (gath.at[:, :, :, pl.ds(0, OWN)], codes_out),
            (key_v, key_out),
            (nm_v, master_out),
            (nmom_v, momentum_out),
            (scales_b, scales_out),
        ))
    ]
    for copy in copies[:-1]:
        copy.start()
    scales_b[...] = scales_v[...].astype(BF16)
    copies[-1].start()
    for copy in copies:
        copy.wait()


def local(activations, key_weight, key_cotangent, grad_codes, grad_scales, master, momentum):
    anywhere, in_hbm = pl.BlockSpec(memory_space=pl.ANY), pl.BlockSpec(memory_space=pltpu.HBM)
    in_vmem = pl.BlockSpec(memory_space=pltpu.VMEM)
    dma = pltpu.SemaphoreType.DMA
    results = pl.pallas_call(
        kernel,
        out_shape=(
            pltpu.VMEM((TOK, KW), BF16),
            pltpu.VMEM((DEPTH, KW), BF16),
            pltpu.VMEM((OWN, 128), F32),
            pltpu.VMEM((OWN, 128), F32),
            pltpu.VMEM((4, 4, 4, 128, 128), BF16),
            pltpu.VMEM((CODE_ROWS // 128, 128), F32),
        ),
        in_specs=[in_hbm] * 7,
        out_specs=(in_vmem,) * 6,
        scratch_shapes=[
            pltpu.VMEM((2 * TOK, DEPTH), BF16),
            pltpu.VMEM((2 * TOK, DEPTH), BF16),
            pltpu.VMEM((2 * TOK, KW), BF16),
            pltpu.VMEM((2 * TOK, KW), BF16),
            pltpu.VMEM((2 * TOK, KW), BF16),
            pltpu.VMEM((DEPTH, KW), BF16),
            pltpu.VMEM((CODE_ROWS, 128), BF16),
            pltpu.VMEM((1, CODE_ROWS), BF16),
            pltpu.VMEM((OWN, 128), F32),
            pltpu.VMEM((OWN, 128), F32),
            pltpu.VMEM((2 * TOK, KW), F32),
            pltpu.VMEM((TOK, KW), F32),
            pltpu.VMEM((2 * TOK, KW), F32),
            pltpu.VMEM((TOK, KW), F32),
            pltpu.VMEM((TOK, KW), BF16),
            pltpu.VMEM((TOK, KW), BF16),
            pltpu.VMEM((DEPTH, KW), F32),
            pltpu.VMEM((4, QUARTER, 128), BF16),
            pltpu.VMEM((3, QUARTER, 128), BF16),
            pltpu.VMEM((4, 4, OWN, 128), BF16),
            pltpu.VMEM((3, 4, OWN, 128), BF16),
            pltpu.VMEM((4, OWN, 128), BF16),
            pltpu.VMEM((3, OWN, 128), BF16),
            dma((7,)),
            dma((2 * NU,)), dma((2 * NU,)),
            dma((5,)), dma((5,)),
            dma((NQ,)), dma((NQ,)),
            dma((NQ,)), dma((NQ,)),
            dma((9,)), dma((9,)),
            dma((9,)), dma((9,)),
        ],
        compiler_params=pltpu.CompilerParams(
            collective_id=0, has_side_effects=True, vmem_limit_bytes=58 * 2**20
        ),
    )(activations, key_weight[0], key_cotangent, grad_codes[0], grad_scales, master, momentum)
    key_rows, weight_grad, new_master, new_momentum, codes, scales = pl.pallas_call(
        write,
        out_shape=(
            jax.ShapeDtypeStruct((TOK, KW), BF16),
            jax.ShapeDtypeStruct((DEPTH, KW), BF16),
            jax.ShapeDtypeStruct((OWN, 128), F32),
            jax.ShapeDtypeStruct((OWN, 128), F32),
            jax.ShapeDtypeStruct((4, 4, 4, OWN, 128), BF16),
            jax.ShapeDtypeStruct((CODE_ROWS // 128, 128), BF16),
        ),
        in_specs=[in_vmem] * 6,
        out_specs=(anywhere,) * 6,
        scratch_shapes=[pltpu.VMEM((CODE_ROWS // 128, 128), BF16), dma((6,))],
        compiler_params=pltpu.CompilerParams(vmem_limit_bytes=2 * 2**20),
    )(*[pltpu.with_memory_space_constraint(v, pltpu.VMEM) for v in results])
    new_codes, new_scales = codes.reshape(CODE_ROWS, 128), scales.reshape(CODE_ROWS)
    return (key_rows, weight_grad[None], new_master, new_momentum, new_codes, new_scales)


def solution(mesh):
    return jax.shard_map(
        local,
        mesh=mesh,
        in_specs=(
            P(("replica", "fsdp"), None),
            P("replica", "fsdp", None),
            P(("replica", "fsdp"), None),
            P("replica", "fsdp", None),
            P("replica", "fsdp"),
            P(("fsdp", "replica"), None),
            P(("fsdp", "replica"), None),
        ),
        out_specs=(
            P(("replica", "fsdp"), None),
            P("replica", "fsdp", None),
            P(("fsdp", "replica"), None),
            P(("fsdp", "replica"), None),
            P("fsdp", None),
            P("fsdp"),
        ),
        check_vma=False,
    )
```

```python
import jax
import jax.numpy as jnp
from jax import lax
from jax.experimental import pallas as pl
from jax.experimental.pallas import tpu as pltpu
from jax.sharding import PartitionSpec as P

MESH = pl.DeviceIdType.MESH
F32, BF16 = jnp.float32, jnp.bfloat16

TOK, DEPTH, KW = 256, 2048, 512
CODE_ROWS, OWN = 7168, 112
QUARTER = CODE_ROWS // 4
UNIT, EARLY, LATE, LAST, NARROW = 16, 4, 4, 3, 8
NU = TOK // UNIT
CHUNKS = ((0, 64), (64, 64), (128, 64), (192, 48), (240, 16))
NQ = len(CHUNKS)
HALVES = [(u, k) for u in range(NU) for k in range(2)]
ORDER = HALVES[:8] + ["c"] + HALVES[8:]
PUMPS = (2, 0, 2, 2, 2, 2, 1, 4, 4, 3, 3, 3)


def kernel(
    act, weight, cot, codes, scales, master, momentum,
    key_b, grad_b, nm_v, nmom_v, gath, scales_b,
    x_loc, x_rem, c_loc, c_rem, c_mix, w_v, codes_v, scales_v, master_v, momentum_v,
    p_loc, p_sib, p_rem, p_ex, ret_s, ret_r, grad_f,
    prod, recv_x, s_y, recv_y, s_z, recv_z,
    sem_in, sem_xs, sem_xr, sem_sib_s, sem_sib_r, sem_ex_s, sem_ex_r, sem_ret_s, sem_ret_r,
    sem_rs_s, sem_rs_r, sem_ag_s, sem_ag_r, token,
):
    r = lax.axis_index("replica")
    f = lax.axis_index("fsdp")
    x, zl, y = r // 16, (r // 4) % 4, r % 4
    zh, c = f // 2, f % 2
    sib = (r, zh * 2 + (1 - c))
    far = [(r, (1 - zh) * 2 + k) for k in range(2)]
    far_same = (r, (1 - zh) * 2 + c)
    px = [(((x + k) % 4) * 16 + zl * 4 + y, f) for k in range(1, 4)]
    pz = [(x * 16 + ((zl + k) % 4) * 4 + y, f) for k in range(1, 4)]
    py = [(x * 16 + zl * 4 + (y + k) % 4, f) for k in range(1, 4)]

    def columns(owner):
        return pl.ds(pl.multiple_of(owner * DEPTH, DEPTH), DEPTH)

    def remote(src, dst, ssem, rsem, to):
        copy = pltpu.make_async_remote_copy(src, dst, ssem, rsem, device_id=to, device_id_type=MESH)
        copy.start()
        return copy

    def local_copy(src, dst, sem):
        copy = pltpu.make_async_copy(src, dst, sem)
        copy.start()
        return copy

    in_codes = local_copy(codes, codes_v, sem_in.at[0])
    in_scales = local_copy(scales, scales_v, sem_in.at[1])
    in_x = local_copy(act.at[:, columns(f)], x_loc.at[pl.ds(0, TOK)], sem_in.at[2])
    in_w = local_copy(weight, w_v, sem_in.at[3])
    in_c = local_copy(cot, c_loc.at[pl.ds(0, TOK)], sem_in.at[4])
    in_master = local_copy(master, master_v, sem_in.at[5])
    in_momentum = local_copy(momentum, momentum_v, sem_in.at[6])

    rivals = [pz[1], (pz[1][0], far_same[1])]
    peers = [sib] + far + px + py + pz + [rivals[1]]
    barrier = pltpu.get_barrier_semaphore()
    for peer in peers:
        pl.semaphore_signal(barrier, inc=1, device_id=peer, device_id_type=MESH)
    pl.semaphore_wait(barrier, len(peers))

    far_c, issued, sent = [], [], []

    def send_far(item):
        if item == "c":
            copy = remote(cot, c_rem.at[pl.ds(c * TOK, TOK)], sem_sib_s.at[2], sem_sib_r.at[2], far_same)
            far_c.append(copy)
            return copy
        u, k = item
        start, rows = next(chunk for chunk in CHUNKS if chunk[0] <= u * UNIT < sum(chunk))
        return remote(
            act.at[pl.ds(u * UNIT, UNIT), columns((1 - zh) * 2 + k)],
            x_rem.at[pl.ds(start + u * UNIT + c * rows, UNIT)],
            sem_xs.at[2 * u + k], sem_xr.at[2 * u + c], far[k],
        )

    def step_done():
        issued[len(sent)].wait_send()
        sent.append(len(sent))
        if len(sent) > len(ORDER) - LAST:
            return
        for i, peer in enumerate(rivals):
            pl.semaphore_signal(token.at[i], inc=1, device_id=peer, device_id_type=MESH)
        for i in range(2):
            pl.semaphore_wait(token.at[i], 1)

    def pump(steps, window=LATE):
        for _ in range(min(steps, len(ORDER) - len(issued))):
            if len(issued) >= len(ORDER) - NARROW:
                window = LAST
            while len(sent) + window <= len(issued):
                step_done()
            issued.append(send_far(ORDER[len(issued)]))

    pump(EARLY, EARLY)
    sib_x = remote(act.at[:, columns(zh * 2 + (1 - c))], x_loc.at[pl.ds(TOK, TOK)], sem_sib_s.at[0], sem_sib_r.at[0], sib)
    sib_c = remote(cot, c_loc.at[pl.ds(TOK, TOK)], sem_sib_s.at[1], sem_sib_r.at[1], sib)

    in_codes.wait()
    in_scales.wait()
    eye = lax.broadcasted_iota(jnp.int32, (128, 128), 0) == lax.broadcasted_iota(jnp.int32, (128, 128), 1)
    rs_x = []
    for k in (1, 3, 2, 0):
        base = ((x + k) % 4) * QUARTER

        def term(b, carry, k=k, base=base):
            at = pl.multiple_of(base + b * 128, 128)
            row = scales_v[:, pl.ds(at, 128)].astype(F32)
            diagonal = jnp.where(eye, jnp.broadcast_to(row, (128, 128)), 0.0).astype(BF16)
            block = jnp.dot(diagonal, codes_v[pl.ds(at, 128), :], preferred_element_type=F32)
            prod[k, pl.ds(pl.multiple_of(b * 128, 128), 128), :] = block.astype(BF16)
            return carry

        lax.fori_loop(0, QUARTER // 128, term, 0)
        if k:
            rs_x.append(remote(prod.at[k], recv_x.at[k - 1], sem_rs_s.at[k - 1], sem_rs_r.at[k - 1], px[k - 1]))
        if k in (2, 3):
            pump(PUMPS[0], EARLY)

    pump(PUMPS[1], EARLY)
    in_x.wait()
    in_w.wait()
    in_c.wait()
    sib_x.wait()
    sib_c.wait()

    def keys_local(b, carry):
        at = pl.ds(pl.multiple_of(b * 128, 128), 128)
        p_loc[at, :] = jnp.dot(x_loc[at, :], w_v[...], preferred_element_type=F32)
        return carry

    lax.fori_loop(0, 2 * TOK // 128, keys_local, 0)
    sib_p = remote(p_loc.at[pl.ds(TOK, TOK)], p_sib, sem_sib_s.at[3], sem_sib_r.at[3], sib)

    pump(PUMPS[2], EARLY)

    def transposed_dot(lhs, rhs):
        return lax.dot_general(lhs, rhs, (((0,), (0,)), ((), ())), preferred_element_type=F32)

    def grad_local(b, carry):
        at = pl.ds(pl.multiple_of(b * 256, 256), 256)
        grad_f[at, :] = transposed_dot(x_loc[:, at], c_loc[...])
        return carry

    lax.fori_loop(0, DEPTH // 256, grad_local, 0)

    pump(PUMPS[3], EARLY)
    def pack_scales():
        lane = lax.broadcasted_iota(jnp.int32, (1, 128), 1)
        for part in range(4):
            rows = [jnp.zeros((1, 128), F32) for _ in range(QUARTER // 128)]
            for owner in range(16):
                at, shift = divmod(owner * OWN, 128)
                row = gath[part, owner // 4, owner % 4, pl.ds(OWN, 16), :][0:1].astype(F32)
                row = jnp.where(lane < OWN, row, 0.0)
                if shift:
                    row = pltpu.roll(row, shift, 1)
                rows[at] += jnp.where(lane >= shift, row, 0.0)
                if shift + OWN > 128:
                    rows[at + 1] += jnp.where(lane < shift, row, 0.0)
            for i, row in enumerate(rows):
                scales_b[pl.ds(part * (QUARTER // 128) + i, 1), :] = row

    def keys_far(q):
        start, rows = CHUNKS[q]
        for u in range(start // UNIT, (start + rows) // UNIT):
            while (u, 1) not in ORDER[: len(issued)]:
                pump(1)
            for k in range(2):
                part = x_rem.at[pl.ds(start + u * UNIT + k * rows, UNIT)]
                pltpu.make_async_copy(part, part, sem_xr.at[2 * u + k]).wait()
        both = pl.ds(2 * start, 2 * rows)
        p_rem[both, :] = jnp.dot(x_rem[both, :], w_v[...], preferred_element_type=F32)
        return remote(
            p_rem.at[pl.ds(2 * start + (1 - c) * rows, rows)], p_ex.at[pl.ds(start, rows)],
            sem_ex_s.at[q], sem_ex_r.at[q], sib,
        )

    def keys_back(q, exchange):
        start, rows = CHUNKS[q]
        exchange.wait()
        at = pl.ds(start, rows)
        mine = p_rem[pl.ds(pl.multiple_of(2 * start + c * rows, rows), rows), :]
        ret_s[at, :] = (mine + p_ex[at, :]).astype(BF16)
        return remote(ret_s.at[at], ret_r.at[at], sem_ret_s.at[q], sem_ret_r.at[q], far_same)

    def grad_far(q):
        start, rows = CHUNKS[q]
        both = pl.ds(2 * start, 2 * rows)

        def tile(b, carry):
            at = pl.ds(pl.multiple_of(b * 256, 256), 256)
            total = grad_f[at, :] + transposed_dot(x_rem[both, at], c_mix[both, :])
            if q < NQ - 1:
                grad_f[at, :] = total
            else:
                grad_b[at, :] = total.astype(BF16)
            return carry

        lax.fori_loop(0, DEPTH // 256, tile, 0)

    for copy in rs_x:
        copy.wait()

    def sum_x(b, carry):
        at = pl.ds(pl.multiple_of(b * OWN, 16), OWN)
        total = prod[0, at, :].astype(F32)
        for k in range(3):
            total += recv_x[k, at, :].astype(F32)
        s_y[b // 4, b % 4] = total.astype(BF16)
        return carry

    lax.fori_loop(0, 16, sum_x, 0)
    rs_y = [
        remote(s_y.at[:, (y + k) % 4], recv_y.at[k - 1], sem_rs_s.at[2 + k], sem_rs_r.at[2 + k], py[k - 1])
        for k in range(1, 4)
    ]
    pump(PUMPS[4], EARLY)
    for copy in rs_y:
        copy.wait()

    def sum_y(b, carry):
        total = s_y[b, y].astype(F32)
        for k in range(3):
            total += recv_y[k, b].astype(F32)
        s_z[b] = total.astype(BF16)
        return carry

    lax.fori_loop(0, 4, sum_y, 0)
    rs_z = [
        remote(s_z.at[(zl + k) % 4], recv_z.at[k - 1], sem_rs_s.at[5 + k], sem_rs_r.at[5 + k], pz[k - 1])
        for k in range(1, 4)
    ]
    pump(PUMPS[5], EARLY)
    in_master.wait()
    in_momentum.wait()
    for copy in rs_z:
        copy.wait()

    total = s_z[zl].astype(F32)
    for k in range(3):
        total += recv_z[k].astype(F32)
    outer = total / 64
    new_momentum = 0.9 * momentum_v[...] + outer
    new_master = master_v[...] - 0.7 * (outer + 0.9 * new_momentum)
    nmom_v[...] = new_momentum
    nm_v[...] = new_master
    largest = jnp.max(jnp.abs(new_master), axis=1, keepdims=True)
    scale = (largest + 1e-06).astype(BF16).astype(F32)
    gath[x, zl, y, 0:OWN, :] = (new_master / scale).astype(BF16)
    corner = lax.broadcasted_iota(jnp.int32, (OWN, 128), 0) == lax.broadcasted_iota(jnp.int32, (OWN, 128), 1)
    row = jnp.sum(jnp.where(corner, jnp.broadcast_to(scale, (OWN, 128)), 0.0), axis=0, keepdims=True)
    gath[x, zl, y, OWN:128, :] = jnp.broadcast_to(row, (128 - OWN, 128)).astype(BF16)

    ag_z = [
        remote(gath.at[x, zl, y], gath.at[x, zl, y], sem_ag_s.at[k - 1], sem_ag_r.at[k - 1], pz[k - 1])
        for k in range(1, 4)
    ]
    pump(PUMPS[6], EARLY)
    returned = [keys_back(0, keys_far(0))]
    for copy in ag_z:
        copy.wait()
    ag_y = [
        remote(gath.at[x, :, y], gath.at[x, :, y], sem_ag_s.at[2 + k], sem_ag_r.at[2 + k], py[k - 1])
        for k in range(1, 4)
    ]
    pump(PUMPS[7])
    for copy in ag_y:
        copy.wait()
    ag_x = []

    def gather_x(k):
        ag_x.append(remote(gath.at[x], gath.at[x], sem_ag_s.at[5 + k], sem_ag_r.at[5 + k], px[k - 1]))

    gather_x(2)
    pump(PUMPS[8])
    returned.append(keys_back(1, keys_far(1)))
    gather_x(1)
    far_c[0].wait_recv()
    share_c = remote(
        c_rem.at[pl.ds(c * TOK, TOK)], c_rem.at[pl.ds(c * TOK, TOK)], sem_sib_s.at[4], sem_sib_r.at[4], sib
    )
    pump(PUMPS[9])
    share_c.wait()
    for q, (start, rows) in enumerate(CHUNKS):
        for k in range(2):
            c_mix[pl.ds(2 * start + k * rows, rows), :] = c_rem[pl.ds(k * TOK + start, rows), :]
    grad_far(0)
    pump(PUMPS[10])
    gather_x(3)
    grad_far(1)
    pump(PUMPS[11])
    returned.append(keys_back(2, keys_far(2)))
    grad_far(2)
    for q in range(3, NQ):
        returned.append(keys_back(q, keys_far(q)))
        grad_far(q)
    while len(sent) < len(issued):
        step_done()
    sib_p.wait()
    for copy in ag_x:
        copy.wait()
    pack_scales()

    for q, (start, rows) in enumerate(CHUNKS):
        returned[q].wait()
        at = pl.ds(start, rows)
        key_b[at, :] = (p_loc[at, :] + p_sib[at, :] + ret_r[at, :].astype(F32)).astype(BF16)


def write(key_v, grad_v, nm_v, nmom_v, gath, scales_v, key_out, grad_out, master_out, momentum_out, codes_out, scales_out, scales_b, sem):
    copies = [
        pltpu.make_async_copy(src, dst, sem.at[i])
        for i, (src, dst) in enumerate((
            (grad_v, grad_out),
            (gath.at[:, :, :, pl.ds(0, OWN)], codes_out),
            (key_v, key_out),
            (nm_v, master_out),
            (nmom_v, momentum_out),
            (scales_b, scales_out),
        ))
    ]
    for copy in copies[:-1]:
        copy.start()
    scales_b[...] = scales_v[...].astype(BF16)
    copies[-1].start()
    for copy in copies:
        copy.wait()


def local(activations, key_weight, key_cotangent, grad_codes, grad_scales, master, momentum):
    anywhere, in_hbm = pl.BlockSpec(memory_space=pl.ANY), pl.BlockSpec(memory_space=pltpu.HBM)
    in_vmem = pl.BlockSpec(memory_space=pltpu.VMEM)
    dma = pltpu.SemaphoreType.DMA
    results = pl.pallas_call(
        kernel,
        out_shape=(
            pltpu.VMEM((TOK, KW), BF16),
            pltpu.VMEM((DEPTH, KW), BF16),
            pltpu.VMEM((OWN, 128), F32),
            pltpu.VMEM((OWN, 128), F32),
            pltpu.VMEM((4, 4, 4, 128, 128), BF16),
            pltpu.VMEM((CODE_ROWS // 128, 128), F32),
        ),
        in_specs=[in_hbm] * 7,
        out_specs=(in_vmem,) * 6,
        scratch_shapes=[
            pltpu.VMEM((2 * TOK, DEPTH), BF16),
            pltpu.VMEM((2 * TOK, DEPTH), BF16),
            pltpu.VMEM((2 * TOK, KW), BF16),
            pltpu.VMEM((2 * TOK, KW), BF16),
            pltpu.VMEM((2 * TOK, KW), BF16),
            pltpu.VMEM((DEPTH, KW), BF16),
            pltpu.VMEM((CODE_ROWS, 128), BF16),
            pltpu.VMEM((1, CODE_ROWS), BF16),
            pltpu.VMEM((OWN, 128), F32),
            pltpu.VMEM((OWN, 128), F32),
            pltpu.VMEM((2 * TOK, KW), F32),
            pltpu.VMEM((TOK, KW), F32),
            pltpu.VMEM((2 * TOK, KW), F32),
            pltpu.VMEM((TOK, KW), F32),
            pltpu.VMEM((TOK, KW), BF16),
            pltpu.VMEM((TOK, KW), BF16),
            pltpu.VMEM((DEPTH, KW), F32),
            pltpu.VMEM((4, QUARTER, 128), BF16),
            pltpu.VMEM((3, QUARTER, 128), BF16),
            pltpu.VMEM((4, 4, OWN, 128), BF16),
            pltpu.VMEM((3, 4, OWN, 128), BF16),
            pltpu.VMEM((4, OWN, 128), BF16),
            pltpu.VMEM((3, OWN, 128), BF16),
            dma((7,)),
            dma((2 * NU,)), dma((2 * NU,)),
            dma((5,)), dma((5,)),
            dma((NQ,)), dma((NQ,)),
            dma((NQ,)), dma((NQ,)),
            dma((9,)), dma((9,)),
            dma((9,)), dma((9,)),
            pltpu.SemaphoreType.REGULAR((2,)),
        ],
        compiler_params=pltpu.CompilerParams(
            collective_id=0, has_side_effects=True, vmem_limit_bytes=58 * 2**20
        ),
    )(activations, key_weight[0], key_cotangent, grad_codes[0], grad_scales, master, momentum)
    key_rows, weight_grad, new_master, new_momentum, codes, scales = pl.pallas_call(
        write,
        out_shape=(
            jax.ShapeDtypeStruct((TOK, KW), BF16),
            jax.ShapeDtypeStruct((DEPTH, KW), BF16),
            jax.ShapeDtypeStruct((OWN, 128), F32),
            jax.ShapeDtypeStruct((OWN, 128), F32),
            jax.ShapeDtypeStruct((4, 4, 4, OWN, 128), BF16),
            jax.ShapeDtypeStruct((CODE_ROWS // 128, 128), BF16),
        ),
        in_specs=[in_vmem] * 6,
        out_specs=(anywhere,) * 6,
        scratch_shapes=[pltpu.VMEM((CODE_ROWS // 128, 128), BF16), dma((6,))],
        compiler_params=pltpu.CompilerParams(vmem_limit_bytes=2 * 2**20),
    )(*[pltpu.with_memory_space_constraint(v, pltpu.VMEM) for v in results])
    new_codes, new_scales = codes.reshape(CODE_ROWS, 128), scales.reshape(CODE_ROWS)
    return (key_rows, weight_grad[None], new_master, new_momentum, new_codes, new_scales)


def solution(mesh):
    return jax.shard_map(
        local,
        mesh=mesh,
        in_specs=(
            P(("replica", "fsdp"), None),
            P("replica", "fsdp", None),
            P(("replica", "fsdp"), None),
            P("replica", "fsdp", None),
            P("replica", "fsdp"),
            P(("fsdp", "replica"), None),
            P(("fsdp", "replica"), None),
        ),
        out_specs=(
            P(("replica", "fsdp"), None),
            P("replica", "fsdp", None),
            P(("fsdp", "replica"), None),
            P(("fsdp", "replica"), None),
            P("fsdp", None),
            P("fsdp"),
        ),
        check_vma=False,
    )
```

```python
import jax
import jax.numpy as jnp
from jax import lax
from jax.experimental import pallas as pl
from jax.experimental.pallas import tpu as pltpu
from jax.sharding import PartitionSpec as P

MESH = pl.DeviceIdType.MESH
F32, BF16 = jnp.float32, jnp.bfloat16

TOK, DEPTH, KW = 256, 2048, 512
CODE_ROWS, OWN = 7168, 112
QUARTER = CODE_ROWS // 4
UNIT, EARLY, LATE, LAST, NARROW = 16, 4, 4, 3, 8
NU = TOK // UNIT
CHUNKS = ((0, 64), (64, 64), (128, 64), (192, 48), (240, 16))
NQ = len(CHUNKS)
HALVES = [(u, k) for u in range(NU) for k in range(2)]
ORDER = HALVES[:8] + ["c"] + HALVES[8:]
PUMPS = (2, 0, 2, 2, 2, 2, 1, 4, 4, 3, 3, 3)


def kernel(
    act, weight, cot, codes, scales, master, momentum,
    key_b, grad_b, nm_v, nmom_v, gath, scales_b,
    x_loc, x_rem, c_loc, c_rem, c_mix, w_v, codes_v, scales_v, master_v, momentum_v,
    p_loc, p_sib, p_rem, p_ex, ret_s, ret_r, grad_f,
    prod, recv_x, s_y, recv_y, s_z, recv_z,
    sem_in, sem_xs, sem_xr, sem_sib_s, sem_sib_r, sem_ex_s, sem_ex_r, sem_ret_s, sem_ret_r,
    sem_rs_s, sem_rs_r, sem_ag_s, sem_ag_r, token,
):
    r = lax.axis_index("replica")
    f = lax.axis_index("fsdp")
    x, zl, y = r // 16, (r // 4) % 4, r % 4
    zh, c = f // 2, f % 2
    sib = (r, zh * 2 + (1 - c))
    far = [(r, (1 - zh) * 2 + k) for k in range(2)]
    far_same = (r, (1 - zh) * 2 + c)
    px = [(((x + k) % 4) * 16 + zl * 4 + y, f) for k in range(1, 4)]
    pz = [(x * 16 + ((zl + k) % 4) * 4 + y, f) for k in range(1, 4)]
    py = [(x * 16 + zl * 4 + (y + k) % 4, f) for k in range(1, 4)]

    def columns(owner):
        return pl.ds(pl.multiple_of(owner * DEPTH, DEPTH), DEPTH)

    def remote(src, dst, ssem, rsem, to):
        copy = pltpu.make_async_remote_copy(src, dst, ssem, rsem, device_id=to, device_id_type=MESH)
        copy.start()
        return copy

    def local_copy(src, dst, sem):
        copy = pltpu.make_async_copy(src, dst, sem)
        copy.start()
        return copy

    in_codes = local_copy(codes, codes_v, sem_in.at[0])
    in_scales = local_copy(scales, scales_v, sem_in.at[1])
    in_x = local_copy(act.at[:, columns(f)], x_loc.at[pl.ds(0, TOK)], sem_in.at[2])
    in_w = local_copy(weight, w_v, sem_in.at[3])
    in_c = local_copy(cot, c_loc.at[pl.ds(0, TOK)], sem_in.at[4])
    in_master = local_copy(master, master_v, sem_in.at[5])
    in_momentum = local_copy(momentum, momentum_v, sem_in.at[6])

    rivals = [pz[1], (pz[1][0], far_same[1])]
    peers = [sib] + far + px + py + pz + [rivals[1]]
    barrier = pltpu.get_barrier_semaphore()
    for peer in peers:
        pl.semaphore_signal(barrier, inc=1, device_id=peer, device_id_type=MESH)
    pl.semaphore_wait(barrier, len(peers))

    far_c, issued, sent = [], [], []

    def send_far(item):
        if item == "c":
            copy = remote(cot, c_rem.at[pl.ds(c * TOK, TOK)], sem_sib_s.at[2], sem_sib_r.at[2], far_same)
            far_c.append(copy)
            return copy
        u, k = item
        start, rows = next(chunk for chunk in CHUNKS if chunk[0] <= u * UNIT < sum(chunk))
        return remote(
            act.at[pl.ds(u * UNIT, UNIT), columns((1 - zh) * 2 + k)],
            x_rem.at[pl.ds(start + u * UNIT + c * rows, UNIT)],
            sem_xs.at[2 * u + k], sem_xr.at[2 * u + c], far[k],
        )

    def step_done():
        issued[len(sent)].wait_send()
        sent.append(len(sent))
        if len(sent) > len(ORDER) - LAST:
            return
        for i, peer in enumerate(rivals):
            pl.semaphore_signal(token.at[i], inc=1, device_id=peer, device_id_type=MESH)
        for i in range(2):
            pl.semaphore_wait(token.at[i], 1)

    def pump(steps, window=LATE):
        for _ in range(min(steps, len(ORDER) - len(issued))):
            if len(issued) >= len(ORDER) - NARROW:
                window = LAST
            while len(sent) + window <= len(issued):
                step_done()
            issued.append(send_far(ORDER[len(issued)]))

    pump(EARLY, EARLY)
    sib_x = remote(act.at[:, columns(zh * 2 + (1 - c))], x_loc.at[pl.ds(TOK, TOK)], sem_sib_s.at[0], sem_sib_r.at[0], sib)
    sib_c = remote(cot, c_loc.at[pl.ds(TOK, TOK)], sem_sib_s.at[1], sem_sib_r.at[1], sib)

    in_codes.wait()
    in_scales.wait()
    eye = lax.broadcasted_iota(jnp.int32, (128, 128), 0) == lax.broadcasted_iota(jnp.int32, (128, 128), 1)
    rs_x = []
    for k in (1, 3, 2, 0):
        base = ((x + k) % 4) * QUARTER

        def term(b, carry, k=k, base=base):
            at = pl.multiple_of(base + b * 128, 128)
            row = scales_v[:, pl.ds(at, 128)].astype(F32)
            diagonal = jnp.where(eye, jnp.broadcast_to(row, (128, 128)), 0.0).astype(BF16)
            block = jnp.dot(diagonal, codes_v[pl.ds(at, 128), :], preferred_element_type=F32)
            prod[k, pl.ds(pl.multiple_of(b * 128, 128), 128), :] = block.astype(BF16)
            return carry

        lax.fori_loop(0, QUARTER // 128, term, 0)
        if k:
            rs_x.append(remote(prod.at[k], recv_x.at[k - 1], sem_rs_s.at[k - 1], sem_rs_r.at[k - 1], px[k - 1]))
        if k in (2, 3):
            pump(PUMPS[0], EARLY)

    pump(PUMPS[1], EARLY)
    in_x.wait()
    in_w.wait()
    in_c.wait()
    sib_x.wait()
    sib_c.wait()

    def keys_local(b, carry):
        at = pl.ds(pl.multiple_of(b * 128, 128), 128)
        p_loc[at, :] = jnp.dot(x_loc[at, :], w_v[...], preferred_element_type=F32)
        return carry

    lax.fori_loop(0, 2 * TOK // 128, keys_local, 0)
    sib_p = remote(p_loc.at[pl.ds(TOK, TOK)], p_sib, sem_sib_s.at[3], sem_sib_r.at[3], sib)

    pump(PUMPS[2], EARLY)

    def transposed_dot(lhs, rhs):
        return lax.dot_general(lhs, rhs, (((0,), (0,)), ((), ())), preferred_element_type=F32)

    def grad_local(b, carry):
        at = pl.ds(pl.multiple_of(b * 256, 256), 256)
        grad_f[at, :] = transposed_dot(x_loc[:, at], c_loc[...])
        return carry

    lax.fori_loop(0, DEPTH // 256, grad_local, 0)

    pump(PUMPS[3], EARLY)
    def pack_scales():
        lane = lax.broadcasted_iota(jnp.int32, (1, 128), 1)
        for part in range(4):
            rows = [jnp.zeros((1, 128), F32) for _ in range(QUARTER // 128)]
            for owner in range(16):
                at, shift = divmod(owner * OWN, 128)
                row = gath[part, owner // 4, owner % 4, pl.ds(OWN, 16), :][0:1].astype(F32)
                row = jnp.where(lane < OWN, row, 0.0)
                if shift:
                    row = pltpu.roll(row, shift, 1)
                rows[at] += jnp.where(lane >= shift, row, 0.0)
                if shift + OWN > 128:
                    rows[at + 1] += jnp.where(lane < shift, row, 0.0)
            for i, row in enumerate(rows):
                scales_b[pl.ds(part * (QUARTER // 128) + i, 1), :] = row

    def keys_far(q):
        start, rows = CHUNKS[q]
        for u in range(start // UNIT, (start + rows) // UNIT):
            while (u, 1) not in ORDER[: len(issued)]:
                pump(1)
            for k in range(2):
                part = x_rem.at[pl.ds(start + u * UNIT + k * rows, UNIT)]
                pltpu.make_async_copy(part, part, sem_xr.at[2 * u + k]).wait()
        both = pl.ds(2 * start, 2 * rows)
        p_rem[both, :] = jnp.dot(x_rem[both, :], w_v[...], preferred_element_type=F32)
        return remote(
            p_rem.at[pl.ds(2 * start + (1 - c) * rows, rows)], p_ex.at[pl.ds(start, rows)],
            sem_ex_s.at[q], sem_ex_r.at[q], sib,
        )

    def keys_back(q, exchange):
        start, rows = CHUNKS[q]
        exchange.wait()
        at = pl.ds(start, rows)
        mine = p_rem[pl.ds(pl.multiple_of(2 * start + c * rows, rows), rows), :]
        ret_s[at, :] = (mine + p_ex[at, :]).astype(BF16)
        return remote(ret_s.at[at], ret_r.at[at], sem_ret_s.at[q], sem_ret_r.at[q], far_same)

    def grad_far(start, stop):
        both = pl.ds(start, stop - start)

        def tile(b, carry):
            at = pl.ds(pl.multiple_of(b * 256, 256), 256)
            total = grad_f[at, :] + transposed_dot(x_rem[both, at], c_mix[both, :])
            if stop < 2 * TOK:
                grad_f[at, :] = total
            else:
                grad_b[at, :] = total.astype(BF16)
            return carry

        lax.fori_loop(0, DEPTH // 256, tile, 0)

    for copy in rs_x:
        copy.wait()

    def sum_x(b, carry):
        at = pl.ds(pl.multiple_of(b * OWN, 16), OWN)
        total = prod[0, at, :].astype(F32)
        for k in range(3):
            total += recv_x[k, at, :].astype(F32)
        s_y[b // 4, b % 4] = total.astype(BF16)
        return carry

    lax.fori_loop(0, 16, sum_x, 0)
    rs_y = [
        remote(s_y.at[:, (y + k) % 4], recv_y.at[k - 1], sem_rs_s.at[2 + k], sem_rs_r.at[2 + k], py[k - 1])
        for k in range(1, 4)
    ]
    pump(PUMPS[4], EARLY)
    for copy in rs_y:
        copy.wait()

    def sum_y(b, carry):
        total = s_y[b, y].astype(F32)
        for k in range(3):
            total += recv_y[k, b].astype(F32)
        s_z[b] = total.astype(BF16)
        return carry

    lax.fori_loop(0, 4, sum_y, 0)
    rs_z = [
        remote(s_z.at[(zl + k) % 4], recv_z.at[k - 1], sem_rs_s.at[5 + k], sem_rs_r.at[5 + k], pz[k - 1])
        for k in range(1, 4)
    ]
    pump(PUMPS[5], EARLY)
    in_master.wait()
    in_momentum.wait()
    for copy in rs_z:
        copy.wait()

    total = s_z[zl].astype(F32)
    for k in range(3):
        total += recv_z[k].astype(F32)
    outer = total / 64
    new_momentum = 0.9 * momentum_v[...] + outer
    new_master = master_v[...] - 0.7 * (outer + 0.9 * new_momentum)
    nmom_v[...] = new_momentum
    nm_v[...] = new_master
    largest = jnp.max(jnp.abs(new_master), axis=1, keepdims=True)
    scale = (largest + 1e-06).astype(BF16).astype(F32)
    gath[x, zl, y, 0:OWN, :] = (new_master / scale).astype(BF16)
    corner = lax.broadcasted_iota(jnp.int32, (OWN, 128), 0) == lax.broadcasted_iota(jnp.int32, (OWN, 128), 1)
    row = jnp.sum(jnp.where(corner, jnp.broadcast_to(scale, (OWN, 128)), 0.0), axis=0, keepdims=True)
    gath[x, zl, y, OWN:128, :] = jnp.broadcast_to(row, (128 - OWN, 128)).astype(BF16)

    ag_z = [
        remote(gath.at[x, zl, y], gath.at[x, zl, y], sem_ag_s.at[k - 1], sem_ag_r.at[k - 1], pz[k - 1])
        for k in range(1, 4)
    ]
    pump(PUMPS[6], EARLY)
    returned = [keys_back(0, keys_far(0))]
    for copy in ag_z:
        copy.wait()
    ag_y = [
        remote(gath.at[x, :, y], gath.at[x, :, y], sem_ag_s.at[2 + k], sem_ag_r.at[2 + k], py[k - 1])
        for k in range(1, 4)
    ]
    pump(PUMPS[7])
    for copy in ag_y:
        copy.wait()
    ag_x = []

    def gather_x(k):
        ag_x.append(remote(gath.at[x], gath.at[x], sem_ag_s.at[5 + k], sem_ag_r.at[5 + k], px[k - 1]))

    gather_x(2)
    pump(PUMPS[8])
    returned.append(keys_back(1, keys_far(1)))
    gather_x(1)
    far_c[0].wait_recv()
    share_c = remote(
        c_rem.at[pl.ds(c * TOK, TOK)], c_rem.at[pl.ds(c * TOK, TOK)], sem_sib_s.at[4], sem_sib_r.at[4], sib
    )
    pump(PUMPS[9])
    share_c.wait()
    for q, (start, rows) in enumerate(CHUNKS):
        for k in range(2):
            c_mix[pl.ds(2 * start + k * rows, rows), :] = c_rem[pl.ds(k * TOK + start, rows), :]
    grad_far(0, 128)
    pump(PUMPS[10])
    gather_x(3)
    grad_far(128, 256)
    pump(PUMPS[11])
    for q in range(2, NQ):
        returned.append(keys_back(q, keys_far(q)))
    grad_far(256, 512)
    while len(sent) < len(issued):
        step_done()
    sib_p.wait()
    for copy in ag_x:
        copy.wait()
    pack_scales()

    for q, (start, rows) in enumerate(CHUNKS):
        returned[q].wait()
        at = pl.ds(start, rows)
        key_b[at, :] = (p_loc[at, :] + p_sib[at, :] + ret_r[at, :].astype(F32)).astype(BF16)


def write(key_v, grad_v, nm_v, nmom_v, gath, scales_v, key_out, grad_out, master_out, momentum_out, codes_out, scales_out, scales_b, sem):
    copies = [
        pltpu.make_async_copy(src, dst, sem.at[i])
        for i, (src, dst) in enumerate((
            (grad_v, grad_out),
            (gath.at[:, :, :, pl.ds(0, OWN)], codes_out),
            (key_v, key_out),
            (nm_v, master_out),
            (nmom_v, momentum_out),
            (scales_b, scales_out),
        ))
    ]
    for copy in copies[:-1]:
        copy.start()
    scales_b[...] = scales_v[...].astype(BF16)
    copies[-1].start()
    for copy in copies:
        copy.wait()


def local(activations, key_weight, key_cotangent, grad_codes, grad_scales, master, momentum):
    anywhere, in_hbm = pl.BlockSpec(memory_space=pl.ANY), pl.BlockSpec(memory_space=pltpu.HBM)
    in_vmem = pl.BlockSpec(memory_space=pltpu.VMEM)
    dma = pltpu.SemaphoreType.DMA
    results = pl.pallas_call(
        kernel,
        out_shape=(
            pltpu.VMEM((TOK, KW), BF16),
            pltpu.VMEM((DEPTH, KW), BF16),
            pltpu.VMEM((OWN, 128), F32),
            pltpu.VMEM((OWN, 128), F32),
            pltpu.VMEM((4, 4, 4, 128, 128), BF16),
            pltpu.VMEM((CODE_ROWS // 128, 128), F32),
        ),
        in_specs=[in_hbm] * 7,
        out_specs=(in_vmem,) * 6,
        scratch_shapes=[
            pltpu.VMEM((2 * TOK, DEPTH), BF16),
            pltpu.VMEM((2 * TOK, DEPTH), BF16),
            pltpu.VMEM((2 * TOK, KW), BF16),
            pltpu.VMEM((2 * TOK, KW), BF16),
            pltpu.VMEM((2 * TOK, KW), BF16),
            pltpu.VMEM((DEPTH, KW), BF16),
            pltpu.VMEM((CODE_ROWS, 128), BF16),
            pltpu.VMEM((1, CODE_ROWS), BF16),
            pltpu.VMEM((OWN, 128), F32),
            pltpu.VMEM((OWN, 128), F32),
            pltpu.VMEM((2 * TOK, KW), F32),
            pltpu.VMEM((TOK, KW), F32),
            pltpu.VMEM((2 * TOK, KW), F32),
            pltpu.VMEM((TOK, KW), F32),
            pltpu.VMEM((TOK, KW), BF16),
            pltpu.VMEM((TOK, KW), BF16),
            pltpu.VMEM((DEPTH, KW), F32),
            pltpu.VMEM((4, QUARTER, 128), BF16),
            pltpu.VMEM((3, QUARTER, 128), BF16),
            pltpu.VMEM((4, 4, OWN, 128), BF16),
            pltpu.VMEM((3, 4, OWN, 128), BF16),
            pltpu.VMEM((4, OWN, 128), BF16),
            pltpu.VMEM((3, OWN, 128), BF16),
            dma((7,)),
            dma((2 * NU,)), dma((2 * NU,)),
            dma((5,)), dma((5,)),
            dma((NQ,)), dma((NQ,)),
            dma((NQ,)), dma((NQ,)),
            dma((9,)), dma((9,)),
            dma((9,)), dma((9,)),
            pltpu.SemaphoreType.REGULAR((2,)),
        ],
        compiler_params=pltpu.CompilerParams(
            collective_id=0, has_side_effects=True, vmem_limit_bytes=58 * 2**20
        ),
    )(activations, key_weight[0], key_cotangent, grad_codes[0], grad_scales, master, momentum)
    key_rows, weight_grad, new_master, new_momentum, codes, scales = pl.pallas_call(
        write,
        out_shape=(
            jax.ShapeDtypeStruct((TOK, KW), BF16),
            jax.ShapeDtypeStruct((DEPTH, KW), BF16),
            jax.ShapeDtypeStruct((OWN, 128), F32),
            jax.ShapeDtypeStruct((OWN, 128), F32),
            jax.ShapeDtypeStruct((4, 4, 4, OWN, 128), BF16),
            jax.ShapeDtypeStruct((CODE_ROWS // 128, 128), BF16),
        ),
        in_specs=[in_vmem] * 6,
        out_specs=(anywhere,) * 6,
        scratch_shapes=[pltpu.VMEM((CODE_ROWS // 128, 128), BF16), dma((6,))],
        compiler_params=pltpu.CompilerParams(vmem_limit_bytes=2 * 2**20),
    )(*[pltpu.with_memory_space_constraint(v, pltpu.VMEM) for v in results])
    new_codes, new_scales = codes.reshape(CODE_ROWS, 128), scales.reshape(CODE_ROWS)
    return (key_rows, weight_grad[None], new_master, new_momentum, new_codes, new_scales)


def solution(mesh):
    return jax.shard_map(
        local,
        mesh=mesh,
        in_specs=(
            P(("replica", "fsdp"), None),
            P("replica", "fsdp", None),
            P(("replica", "fsdp"), None),
            P("replica", "fsdp", None),
            P("replica", "fsdp"),
            P(("fsdp", "replica"), None),
            P(("fsdp", "replica"), None),
        ),
        out_specs=(
            P(("replica", "fsdp"), None),
            P("replica", "fsdp", None),
            P(("fsdp", "replica"), None),
            P(("fsdp", "replica"), None),
            P("fsdp", None),
            P("fsdp"),
        ),
        check_vma=False,
    )
```
